512 devices in a mesh: prow: 8 (over y), pcol: 64 (over x, z, core).
Axes of the slice: x: 4, y: 8, z: 8, core: 2. Of those that a mesh axis runs over, the one named last changes fastest.
Arguments:
- sigma_anc: float32 [6144, 6144], P('prow', 'pcol'), as said below
- panel_top: float32 [6144, 2048], P('prow', 'pcol'), may hold values from -0.3 to 0.3
- pivot_top: float32 [2048, 2048], P('prow', 'pcol'), as said below
- flags_top: int32 [192], replicated, may hold values from 0 to 1, as said below
- panel_kids: float32 [2, 2048, 1024], P(None, 'prow', 'pcol'), may hold values from -0.3 to 0.3
- pivot_kids: float32 [2, 1024, 1024], P(None, 'prow', 'pcol'), as said below
- flags_kids: int32 [2, 64], replicated, may hold values 0 or 1
Outputs:
- cross_top: float32 [2048, 6144], P('prow', 'pcol')
- sigma_top: float32 [2048, 2048], P('prow', 'pcol')
- cross_kids: float32 [2, 1024, 2048], P(None, 'prow', 'pcol')
- sigma_kids: float32 [2, 1024, 1024], P(None, 'prow', 'pcol')
The draws below stay inside these ranges and needn't reach their ends.
Inputs may be any that keep to these rules, and one draw needn't show every extreme that they name: `sigma_anc`: exactly symmetric. `pivot_top`: exactly symmetric. `pivot_kids`: each matrix exactly symmetric. `flags_top`: in each aligned window of 24 consecutive entries at most 16 are 1, and some window has exactly 16.
All inputs are finite; a program needn't handle non-finite values.
Results may differ from the reference program's by a relative error of at most 0.000073.
Values sent between devices are 32-bit elements; how exact they have to be, the bound alone decides.
No kernel may reach another device: no remote copies, remote signals or barrier semaphores. Data moves between devices by JAX's collectives and lax.ppermute only.
A program may use at most 64 MiB of HBM per device.

```python
import math
import jax
import jax.numpy as jnp
from jax import lax

W1 = 2048
W2 = 1024
BLK = 32
ANC = 6144
BLK_OWN = 24
LIVE_TOP = 16
NB_A = 192
NB_K = 64


def symmetric_field(rng_key, order, leading):
    first, second = jax.random.split(rng_key, 2)
    noise = jax.random.normal(first, leading + (order, order), jnp.float32)
    coupling = (noise + jnp.swapaxes(noise, -1, -2)) * (0.5 / math.sqrt(order))
    ident = (jnp.arange(order)[:, None] == jnp.arange(order)[None, :]).astype(jnp.float32)
    diagonal = jax.random.uniform(second, leading + (order,), jnp.float32, 0.5, 2.0)
    return coupling * (1.0 - ident) + ident * diagonal[..., None, :]


def draw_sigma_anc(key, part):
    matrix = symmetric_field(jax.random.fold_in(key, 11), ANC, ())
    return matrix


def draw_pivot_top(key, part):
    matrix = symmetric_field(jax.random.fold_in(key, 21), W1, ())
    return matrix


def draw_pivot_kids(key, part):
    matrix = symmetric_field(jax.random.fold_in(key, 31), W2, (2,))
    return matrix


def draw_flags_top(key, part):
    windows = NB_A // BLK_OWN
    first, second, third = jax.random.split(jax.random.fold_in(key, 41), 3)
    counts = jax.random.randint(first, (windows,), LIVE_TOP // 2, LIVE_TOP + 1)
    picked = jax.random.randint(second, (), 0, windows)
    counts = jnp.where(jnp.arange(windows) == picked, LIVE_TOP, counts)
    ranking = jax.vmap(lambda sub_key: jax.random.permutation(sub_key, BLK_OWN))(jax.random.split(third, windows))
    return (ranking < counts[:, None]).astype(jnp.int32).reshape(-1)


def plant(result, own_key, low, largest):
    dims = result.shape
    place = [jax.random.randint(jax.random.fold_in(own_key, axis), (), 0, dims[axis]) for axis in range(len(dims))]
    result = result.at[tuple(place)].set(low)
    longest = dims.index(max(dims))
    place[longest] = (place[longest] + 1) % dims[longest]
    return result.at[tuple(place)].set(largest)


def steps_of(key, shape, pieces, low, top_value):
    level = 1.0
    for axis_at, blocks in pieces:
        draws = jax.random.uniform(jax.random.fold_in(jax.random.fold_in(key, 6), axis_at), (blocks,), jnp.float32, low / len(pieces), top_value / len(pieces))
        level = level * jnp.repeat(jnp.exp(draws), shape[axis_at] // blocks).reshape((-1,) + (1,) * (len(shape) - 1 - axis_at))
    return level


def bell_draw(rng, extent, deviation, reach, pieces=(), kind=jnp.bfloat16):
    result = deviation * jax.random.normal(rng, extent, jnp.float32)
    if pieces:
        result = result * steps_of(rng, extent, pieces, -0.22, 0.18)
    return jnp.clip(result, -reach, reach).astype(kind)


def setup_inputs(seed: int = 0) -> dict:
    keys = jax.random.split(jax.random.key(seed), 8)
    return {
        "sigma_anc": draw_sigma_anc(jax.random.fold_in(keys[7], 71), 0),
        "panel_top": bell_draw(keys[1], (ANC, W1), 0.05, 0.3, ((0, 8), (1, 64)), jnp.float32),
        "pivot_top": draw_pivot_top(jax.random.fold_in(keys[7], 71), 0),
        "flags_top": draw_flags_top(jax.random.fold_in(keys[7], 71), 0),
        "panel_kids": bell_draw(keys[4], (2, W1, W2), 0.05, 0.3, ((1, 8), (2, 64)), jnp.float32),
        "pivot_kids": draw_pivot_kids(jax.random.fold_in(keys[7], 71), 0),
        "flags_kids": plant((jax.random.randint(keys[6], (2, NB_K), 0, 5) < 3).astype(jnp.int32), jax.random.fold_in(keys[6], 1), 0, 1),
    }


HIGH = lax.Precision.HIGHEST


def reference(sigma_anc, panel_top, pivot_top, flags_top, panel_kids, pivot_kids, flags_kids):
    keep_top = jnp.take(flags_top, jnp.arange(ANC) // BLK).astype(jnp.float32)
    masked_top = panel_top * keep_top[:, None]
    zed_top = jnp.dot(sigma_anc, masked_top, precision=HIGH, preferred_element_type=jnp.float32)
    cross_top = -jnp.transpose(zed_top * keep_top[:, None])
    sigma_top = pivot_top + jnp.dot(jnp.transpose(zed_top), masked_top, precision=HIGH, preferred_element_type=jnp.float32)
    keep_kids = jnp.take(flags_kids, jnp.arange(W1) // BLK, axis=1).astype(jnp.float32)
    masked_kids = panel_kids * keep_kids[:, :, None]
    zed_kids = jnp.einsum("kj,ckw->cjw", sigma_top, masked_kids, precision=HIGH)
    cross_kids = -jnp.transpose(zed_kids * keep_kids[:, :, None], (0, 2, 1))
    sigma_kids = pivot_kids + jnp.einsum("cjw,cjv->cwv", zed_kids, masked_kids, precision=HIGH)
    return cross_top, sigma_top, cross_kids, sigma_kids
```

```python
import jax
import jax.numpy as jnp
from jax import lax
from jax.sharding import Mesh
from jax.sharding import PartitionSpec as P

BLK = 32
LIVE = 16
HIGH = lax.Precision.HIGH
WIN = ("x", "h")
SUB = ("q", "c")


def dot_nt(a, b):
    return lax.dot_general(
        a, b, (((1,), (1,)), ((), ())), precision=HIGH, preferred_element_type=jnp.float32
    )


def pieces(value):
    high = lax.reduce_precision(value, 8, 7)
    rest = value - high
    mid = lax.reduce_precision(rest, 8, 7)
    return [part.astype(jnp.bfloat16) for part in (high, mid, rest - mid)]


def select_exact(value, choice):
    rows = value.shape[0]
    stacked = jnp.concatenate(pieces(value), axis=0)
    picked = lax.dot_general(
        stacked, choice, (((1,), (0,)), ((), ())), preferred_element_type=jnp.float32
    )
    return picked[:rows] + (picked[rows : 2 * rows] + picked[2 * rows :])


def slot_choice(window, block_ids, count):
    order = jnp.arange(window.shape[0])
    rank = jnp.sum(jnp.where(order[None, :] < order[:, None], window[None, :], 0), axis=1)
    slot = jnp.where(window == 1, rank, -1)
    slot_of = jnp.sum(
        jnp.where(block_ids[:, None] == jnp.arange(window.shape[0])[None, :], slot[None, :], 0), axis=1
    )
    slot_of = jnp.broadcast_to(slot_of[:, None], (block_ids.shape[0], BLK)).reshape(-1)
    place = slot_of * BLK + jnp.arange(block_ids.shape[0] * BLK, dtype=jnp.int32) % BLK
    place = jnp.where(slot_of >= 0, place, -1)
    return (place[:, None] == jnp.arange(count, dtype=jnp.int32)[None, :]).astype(jnp.bfloat16)


def swap(value, axis):
    return lax.ppermute(value, axis, [(0, 1), (1, 0)])


def sum_over(parts, axis):
    return jnp.sum(lax.all_to_all(parts, axis, 0, 0, tiled=True), axis=0)


def turn(value, count):
    places = [(i, j) for i in range(count) for j in range(count)]
    for goes in (lambda i, j: ((i + j) % count, j), lambda i, j: (i, (i - j) % count)):
        order = [(i * count + j, goes(i, j)[0] * count + goes(i, j)[1]) for i, j in places]
        value = lax.ppermute(value, ("y",) + WIN, order)
    return value


def in_order(parts, first):
    twice = jnp.concatenate([parts, parts], axis=0)
    return lax.dynamic_slice_in_dim(twice, first, parts.shape[0], 0)


def spread(value, axis):
    copies = jnp.broadcast_to(value[None], (lax.axis_size(axis),) + value.shape)
    return lax.all_to_all(copies, axis, 0, 0, tiled=True)


def gather_sub(rows):
    lines = spread(rows, "q")
    both = lax.all_gather(lines, "c", axis=1)
    return both.reshape((-1,) + rows.shape)


def per_device(sigma_anc, panel_top, pivot_top, flags_top, panel_kids, pivot_kids, flags_kids):
    ny, nx, nh = lax.axis_size("y"), lax.axis_size("x"), lax.axis_size("h")
    nq = lax.axis_size("q")
    y_id, q_id, c_id, h_id = (lax.axis_index(a) for a in ("y", "q", "c", "h"))
    win_id = lax.axis_index("x") * nh + h_id
    sub_id = q_id * 2 + c_id
    anc_own, anc_col = sigma_anc.shape
    per_win = anc_own // BLK
    per_col = anc_col // BLK
    live = LIVE * BLK
    top_col = panel_top.shape[1]
    kid_own = panel_kids.shape[1]
    kid_col = panel_kids.shape[2]

    row_window = lax.dynamic_slice_in_dim(flags_top, y_id * per_win, per_win)
    col_window = lax.dynamic_slice_in_dim(flags_top, win_id * per_win, per_win)
    row_choice = slot_choice(row_window, jnp.arange(per_win), live)
    group = jnp.arange(nq * per_col) // per_col
    within = jnp.arange(nq * per_col) % per_col
    near_choice = slot_choice(col_window, (group * 2 + c_id) * per_col + within, live)
    far_choice = slot_choice(col_window, (group * 2 + 1 - c_id) * per_col + within, live)
    own_choice = slot_choice(col_window, sub_id * per_col + jnp.arange(per_col), live)

    packed = select_exact(jnp.concatenate([sigma_anc.T, panel_top.T], axis=0), row_choice)
    field = packed[:anc_col]
    top_rows = packed[anc_col:]
    kid_blocks = kid_own // BLK
    kid_flags = lax.dynamic_slice_in_dim(flags_kids, y_id * kid_blocks, kid_blocks, 1)
    keep_rows = jnp.repeat(kid_flags, BLK, axis=1).astype(jnp.float32)
    kids = jnp.transpose(panel_kids, (0, 2, 1)) * keep_rows[:, None, :]
    panel = jnp.concatenate([top_rows, kids.reshape(2 * kid_col, kid_own)], axis=1)

    turned = turn(panel, ny)
    other = swap(panel, "h")
    near = lax.all_gather(field, "q", axis=0).reshape(nq * anc_col, live)
    near, other, turned = lax.optimization_barrier((near, other, turned))
    far = swap(near, "c")
    pair = jnp.stack([jnp.where(h_id == 0, panel, other), jnp.where(h_id == 0, other, panel)])
    turned = spread(turned, "y").reshape(ny * top_col, live + kid_own)
    wide = spread(pair, "x").reshape(ny * top_col, live + kid_own)

    top_wide = wide[:, :live]
    zed = select_exact(dot_nt(top_wide, near), near_choice) + select_exact(
        dot_nt(top_wide, far), far_choice
    )
    zed, turned = lax.optimization_barrier((zed, turned))
    zed = sum_over(zed.reshape(ny, top_col, live), "y")
    zed = gather_sub(zed).reshape(-1, live)
    cross_top = -lax.dot_general(
        own_choice, jnp.concatenate(pieces(zed), axis=0), (((1,), (1,)), ((), ())),
        preferred_element_type=jnp.float32,
    ).reshape(anc_col, 3, -1).sum(axis=1)

    part = dot_nt(turned[:, :live], zed)
    sigma_top = pivot_top.T + sum_over(
        in_order(part.reshape(nx * nh, top_col, -1), win_id), WIN
    )

    block = gather_sub(sigma_top).reshape(-1, kid_own)
    part = dot_nt(wide[:, live:], block)
    zed = sum_over(part.reshape(ny, 2 * kid_col, -1), "y")
    zed = gather_sub(zed.reshape(2, kid_col, -1))
    zed = jnp.transpose(zed, (1, 0, 2, 3)).reshape(2, -1, kid_own)
    col_flags = lax.dynamic_slice_in_dim(flags_kids, win_id * kid_blocks + sub_id, 1, 1)
    cross_kids = lax.dynamic_slice_in_dim(zed, sub_id * top_col, top_col, 2)
    cross_kids = -(cross_kids * col_flags.astype(jnp.float32)[:, :, None])

    turned_kids = turned[:, live:].reshape(nx * nh, 2, kid_col, kid_own)
    part = jnp.stack(
        [dot_nt(turned_kids[:, k].reshape(-1, kid_own), zed[k]) for k in range(2)]
    )
    part = jnp.transpose(part.reshape(2, nx * nh, kid_col, -1), (1, 0, 2, 3))
    sigma_kids = jnp.transpose(pivot_kids, (0, 2, 1)) + sum_over(in_order(part, win_id), WIN)
    return (
        cross_top.T,
        sigma_top.T,
        cross_kids,
        jnp.transpose(sigma_kids, (0, 2, 1)),
    )


def solution(mesh):
    fine = Mesh(mesh.devices.reshape(8, 4, 2, 4, 2), ("y", "x", "h", "q", "c"))
    cols = ("x", "h", "q", "c")
    flat = P("y", cols)
    kids = P(None, "y", cols)
    return jax.shard_map(
        per_device,
        mesh=fine,
        in_specs=(flat, flat, flat, P(), kids, kids, P()),
        out_specs=(flat, flat, kids, kids),
        check_vma=False,
    )
```

```python
import jax
import jax.numpy as jnp
from jax import lax
from jax.sharding import Mesh
from jax.sharding import PartitionSpec as P

BLK = 32
LIVE = 16
HIGH = lax.Precision.HIGH
WIN = ("x", "h")
SUB = ("q", "c")


def dot_nt(a, b):
    return lax.dot_general(
        a, b, (((1,), (1,)), ((), ())), precision=HIGH, preferred_element_type=jnp.float32
    )


def pieces(value):
    high = lax.reduce_precision(value, 8, 7)
    rest = value - high
    mid = lax.reduce_precision(rest, 8, 7)
    return [part.astype(jnp.bfloat16) for part in (high, mid, rest - mid)]


def select_exact(value, choice):
    rows = value.shape[0]
    stacked = jnp.concatenate(pieces(value), axis=0)
    picked = lax.dot_general(
        stacked, choice, (((1,), (0,)), ((), ())), preferred_element_type=jnp.float32
    )
    return picked[:rows] + (picked[rows : 2 * rows] + picked[2 * rows :])


def slot_choice(window, block_ids, count):
    order = jnp.arange(window.shape[0])
    rank = jnp.sum(jnp.where(order[None, :] < order[:, None], window[None, :], 0), axis=1)
    slot = jnp.where(window == 1, rank, -1)
    slot_of = jnp.sum(
        jnp.where(block_ids[:, None] == jnp.arange(window.shape[0])[None, :], slot[None, :], 0), axis=1
    )
    slot_of = jnp.broadcast_to(slot_of[:, None], (block_ids.shape[0], BLK)).reshape(-1)
    place = slot_of * BLK + jnp.arange(block_ids.shape[0] * BLK, dtype=jnp.int32) % BLK
    place = jnp.where(slot_of >= 0, place, -1)
    return (place[:, None] == jnp.arange(count, dtype=jnp.int32)[None, :]).astype(jnp.bfloat16)


def swap(value, axis):
    return lax.ppermute(value, axis, [(0, 1), (1, 0)])


def sum_over(parts, axis):
    return jnp.sum(lax.all_to_all(parts, axis, 0, 0, tiled=True), axis=0)


def shift(value, goes, count):
    order = []
    for i in range(count):
        for j in range(count):
            to_y, to_window = goes(i, j)
            order.append((i * count + j, to_y * count + to_window))
    return lax.ppermute(value, ("y",) + WIN, order)


def in_order(parts, first):
    twice = jnp.concatenate([parts, parts], axis=0)
    return lax.dynamic_slice_in_dim(twice, first, parts.shape[0], 0)


def spread(value, axis):
    copies = jnp.broadcast_to(value[None], (lax.axis_size(axis),) + value.shape)
    return lax.all_to_all(copies, axis, 0, 0, tiled=True)


def gather_sub(rows):
    lines = spread(rows, "q")
    both = lax.all_gather(lines, "c", axis=1)
    return both.reshape((-1,) + rows.shape)


def per_device(sigma_anc, panel_top, pivot_top, flags_top, panel_kids, pivot_kids, flags_kids):
    ny, nx, nh = lax.axis_size("y"), lax.axis_size("x"), lax.axis_size("h")
    nq = lax.axis_size("q")
    y_id, q_id, c_id, h_id = (lax.axis_index(a) for a in ("y", "q", "c", "h"))
    win_id = lax.axis_index("x") * nh + h_id
    sub_id = q_id * 2 + c_id
    anc_own, anc_col = sigma_anc.shape
    per_win = anc_own // BLK
    per_col = anc_col // BLK
    live = LIVE * BLK
    top_col = panel_top.shape[1]
    kid_own = panel_kids.shape[1]
    kid_col = panel_kids.shape[2]

    row_window = lax.dynamic_slice_in_dim(flags_top, y_id * per_win, per_win)
    col_window = lax.dynamic_slice_in_dim(flags_top, win_id * per_win, per_win)
    row_choice = slot_choice(row_window, jnp.arange(per_win), live)
    group = jnp.arange(nq * per_col) // per_col
    within = jnp.arange(nq * per_col) % per_col
    near_choice = slot_choice(col_window, (group * 2 + c_id) * per_col + within, live)
    far_choice = slot_choice(col_window, (group * 2 + 1 - c_id) * per_col + within, live)
    own_choice = slot_choice(col_window, sub_id * per_col + jnp.arange(per_col), live)

    packed = select_exact(jnp.concatenate([sigma_anc.T, panel_top.T], axis=0), row_choice)
    field = packed[:anc_col]
    top_rows = packed[anc_col:]
    kid_blocks = kid_own // BLK
    kid_flags = lax.dynamic_slice_in_dim(flags_kids, y_id * kid_blocks, kid_blocks, 1)
    keep_rows = jnp.repeat(kid_flags, BLK, axis=1).astype(jnp.float32)
    kids = jnp.transpose(panel_kids, (0, 2, 1)) * keep_rows[:, None, :]
    panel = jnp.concatenate([top_rows, kids.reshape(2 * kid_col, kid_own)], axis=1)

    kid_rows = lax.all_gather(kids, WIN + SUB, axis=1, tiled=True)
    turned = shift(panel, lambda i, j: ((i + j) % ny, j), ny)
    other = swap(top_rows, "h")
    near = lax.all_gather(field, "q", axis=0).reshape(nq * anc_col, live)
    near, other, turned = lax.optimization_barrier((near, other, turned))
    turned = shift(turned, lambda i, j: (i, (i - j) % ny), ny)
    far = swap(near, "c")
    pair = jnp.stack([jnp.where(h_id == 0, top_rows, other), jnp.where(h_id == 0, other, top_rows)])
    top_wide = spread(pair, "x").reshape(ny * top_col, live)
    top_wide, turned = lax.optimization_barrier((top_wide, turned))
    zed = select_exact(dot_nt(top_wide, near), near_choice) + select_exact(
        dot_nt(top_wide, far), far_choice
    )
    zed = sum_over(zed.reshape(ny, top_col, live), "y")
    zed, turned = lax.optimization_barrier((zed, turned))
    turned = spread(turned, "y").reshape(ny * top_col, live + kid_own)
    zed = lax.all_gather(lax.all_gather(zed, "q", axis=0), "c", axis=1).reshape(-1, live)
    cross_top = -lax.dot_general(
        own_choice, jnp.concatenate(pieces(zed), axis=0), (((1,), (1,)), ((), ())),
        preferred_element_type=jnp.float32,
    ).reshape(anc_col, 3, -1).sum(axis=1)

    part = dot_nt(turned[:, :live], zed)
    sigma_top = pivot_top.T + sum_over(
        in_order(part.reshape(nx * nh, top_col, -1), win_id), WIN
    )

    part = dot_nt(sigma_top, kid_rows.reshape(-1, kid_own)).reshape(top_col, 2, ny, -1)
    zed = sum_over(jnp.transpose(part, (2, 1, 0, 3)), "y")
    col_flags = lax.dynamic_slice_in_dim(flags_kids, win_id * kid_blocks + sub_id, 1, 1)
    cross_kids = -(zed * col_flags.astype(jnp.float32)[:, :, None])

    zed = gather_sub(zed)
    turned_kids = turned[:, live:].reshape(nx * nh, 2, kid_col, kid_own)
    part = jnp.stack(
        [
            lax.dot(
                turned_kids[:, k].reshape(-1, kid_own),
                zed[:, k].reshape(kid_own, -1),
                precision=HIGH,
                preferred_element_type=jnp.float32,
            )
            for k in range(2)
        ]
    )
    part = jnp.transpose(part.reshape(2, nx * nh, kid_col, -1), (1, 0, 2, 3))
    sigma_kids = jnp.transpose(pivot_kids, (0, 2, 1)) + sum_over(in_order(part, win_id), WIN)
    return (
        cross_top.T,
        sigma_top.T,
        jnp.transpose(cross_kids, (0, 2, 1)),
        jnp.transpose(sigma_kids, (0, 2, 1)),
    )


def solution(mesh):
    fine = Mesh(mesh.devices.reshape(8, 4, 2, 4, 2), ("y", "x", "h", "q", "c"))
    cols = ("x", "h", "q", "c")
    flat = P("y", cols)
    kids = P(None, "y", cols)
    return jax.shard_map(
        per_device,
        mesh=fine,
        in_specs=(flat, flat, flat, P(), kids, kids, P()),
        out_specs=(flat, flat, kids, kids),
        check_vma=False,
    )
```

```python
import jax
import jax.numpy as jnp
from jax import lax
from jax.sharding import Mesh
from jax.sharding import PartitionSpec as P

BLK = 32
LIVE = 16
HIGH = lax.Precision.HIGH
WIN = ("x", "h")
SUB = ("q", "c")


def dot_nt(a, b):
    return lax.dot_general(
        a, b, (((1,), (1,)), ((), ())), precision=HIGH, preferred_element_type=jnp.float32
    )


def pieces(value):
    high = lax.reduce_precision(value, 8, 7)
    rest = value - high
    mid = lax.reduce_precision(rest, 8, 7)
    return [part.astype(jnp.bfloat16) for part in (high, mid, rest - mid)]


def select_exact(value, choice):
    rows = value.shape[0]
    stacked = jnp.concatenate(pieces(value), axis=0)
    picked = lax.dot_general(
        stacked, choice, (((1,), (0,)), ((), ())), preferred_element_type=jnp.float32
    )
    return picked[:rows] + (picked[rows : 2 * rows] + picked[2 * rows :])


def slot_choice(window, block_ids, count):
    order = jnp.arange(window.shape[0])
    rank = jnp.sum(jnp.where(order[None, :] < order[:, None], window[None, :], 0), axis=1)
    slot = jnp.where(window == 1, rank, -1)
    slot_of = jnp.sum(
        jnp.where(block_ids[:, None] == jnp.arange(window.shape[0])[None, :], slot[None, :], 0), axis=1
    )
    slot_of = jnp.broadcast_to(slot_of[:, None], (block_ids.shape[0], BLK)).reshape(-1)
    place = slot_of * BLK + jnp.arange(block_ids.shape[0] * BLK, dtype=jnp.int32) % BLK
    place = jnp.where(slot_of >= 0, place, -1)
    return (place[:, None] == jnp.arange(count, dtype=jnp.int32)[None, :]).astype(jnp.bfloat16)


def swap(value, axis):
    return lax.ppermute(value, axis, [(0, 1), (1, 0)])


def sum_over(parts, axis):
    return jnp.sum(lax.all_to_all(parts, axis, 0, 0, tiled=True), axis=0)


def shift(value, goes, count):
    order = []
    for i in range(count):
        for j in range(count):
            to_y, to_window = goes(i, j)
            order.append((i * count + j, to_y * count + to_window))
    return lax.ppermute(value, ("y",) + WIN, order)


def in_order(parts, first):
    twice = jnp.concatenate([parts, parts], axis=0)
    return lax.dynamic_slice_in_dim(twice, first, parts.shape[0], 0)


def spread(value, axis):
    copies = jnp.broadcast_to(value[None], (lax.axis_size(axis),) + value.shape)
    return lax.all_to_all(copies, axis, 0, 0, tiled=True)


def gather_sub(rows):
    lines = spread(rows, "q")
    both = lax.all_gather(lines, "c", axis=1)
    return both.reshape((-1,) + rows.shape)


def per_device(sigma_anc, panel_top, pivot_top, flags_top, panel_kids, pivot_kids, flags_kids):
    ny, nx, nh = lax.axis_size("y"), lax.axis_size("x"), lax.axis_size("h")
    nq = lax.axis_size("q")
    y_id, q_id, c_id, h_id = (lax.axis_index(a) for a in ("y", "q", "c", "h"))
    win_id = lax.axis_index("x") * nh + h_id
    sub_id = q_id * 2 + c_id
    anc_own, anc_col = sigma_anc.shape
    per_win = anc_own // BLK
    per_col = anc_col // BLK
    live = LIVE * BLK
    top_col = panel_top.shape[1]
    kid_own = panel_kids.shape[1]
    kid_col = panel_kids.shape[2]

    row_window = lax.dynamic_slice_in_dim(flags_top, y_id * per_win, per_win)
    col_window = lax.dynamic_slice_in_dim(flags_top, win_id * per_win, per_win)
    row_choice = slot_choice(row_window, jnp.arange(per_win), live)
    group = jnp.arange(nq * per_col) // per_col
    within = jnp.arange(nq * per_col) % per_col
    near_choice = slot_choice(col_window, (group * 2 + c_id) * per_col + within, live)
    far_choice = slot_choice(col_window, (group * 2 + 1 - c_id) * per_col + within, live)
    own_choice = slot_choice(col_window, sub_id * per_col + jnp.arange(per_col), live)

    packed = select_exact(jnp.concatenate([sigma_anc.T, panel_top.T], axis=0), row_choice)
    field = packed[:anc_col]
    top_rows = packed[anc_col:]
    kid_blocks = kid_own // BLK
    kid_flags = lax.dynamic_slice_in_dim(flags_kids, y_id * kid_blocks, kid_blocks, 1)
    keep_rows = jnp.repeat(kid_flags, BLK, axis=1).astype(jnp.float32)
    kids = jnp.transpose(panel_kids, (0, 2, 1)) * keep_rows[:, None, :]
    panel = jnp.concatenate([top_rows, kids.reshape(2 * kid_col, kid_own)], axis=1)

    kid_rows = lax.all_gather(kids, WIN + SUB, axis=1, tiled=True)
    turned = shift(panel, lambda i, j: ((i + j) % ny, j), ny)
    other = swap(top_rows, "h")
    field, other = lax.optimization_barrier((field, other))
    pair = jnp.stack([jnp.where(h_id == 0, top_rows, other), jnp.where(h_id == 0, other, top_rows)])
    top_wide = spread(pair, "x").reshape(ny * top_col, live)
    turned = shift(turned, lambda i, j: (i, (i - j) % ny), ny)
    near = lax.all_gather(field, "q", axis=0).reshape(nq * anc_col, live)
    near, top_wide, turned = lax.optimization_barrier((near, top_wide, turned))
    far = swap(near, "c")
    zed = jnp.concatenate([dot_nt(top_wide, near), dot_nt(top_wide, far)], axis=1)
    zed = select_exact(zed, jnp.concatenate([near_choice, far_choice], axis=0))
    zed = sum_over(zed.reshape(ny, top_col, live), "y")
    zed, turned = lax.optimization_barrier((zed, turned))
    turned = spread(turned, "y").reshape(ny * top_col, live + kid_own)
    zed = lax.all_gather(lax.all_gather(zed, "q", axis=0), "c", axis=1).reshape(-1, live)
    cross_top = -lax.dot_general(
        own_choice, jnp.concatenate(pieces(zed), axis=0), (((1,), (1,)), ((), ())),
        preferred_element_type=jnp.float32,
    ).reshape(anc_col, 3, -1).sum(axis=1)

    part = dot_nt(turned[:, :live], zed)
    part, kid_rows = lax.optimization_barrier((part, kid_rows))
    kid_high, kid_low, _ = pieces(kid_rows.reshape(-1, kid_own))
    kid_terms = jnp.concatenate([kid_high, kid_low, kid_high], axis=1)
    sigma_top = pivot_top.T + sum_over(
        in_order(part.reshape(nx * nh, top_col, -1), win_id), WIN
    )

    top_high, top_low, _ = pieces(sigma_top)
    part = lax.dot_general(
        jnp.concatenate([top_high, top_high, top_low], axis=1),
        kid_terms,
        (((1,), (1,)), ((), ())),
        preferred_element_type=jnp.float32,
    ).reshape(top_col, 2, ny, -1)
    zed = sum_over(jnp.transpose(part, (2, 1, 0, 3)), "y")
    col_flags = lax.dynamic_slice_in_dim(flags_kids, win_id * kid_blocks + sub_id, 1, 1)
    cross_kids = -(zed * col_flags.astype(jnp.float32)[:, :, None])

    zed = gather_sub(zed)
    turned_kids = turned[:, live:].reshape(nx * nh, 2, kid_col, kid_own)
    part = jnp.stack(
        [
            lax.dot(
                turned_kids[:, k].reshape(-1, kid_own),
                zed[:, k].reshape(kid_own, -1),
                precision=HIGH,
                preferred_element_type=jnp.float32,
            )
            for k in range(2)
        ]
    )
    part = jnp.transpose(part.reshape(2, nx * nh, kid_col, -1), (1, 0, 2, 3))
    sigma_kids = jnp.transpose(pivot_kids, (0, 2, 1)) + sum_over(in_order(part, win_id), WIN)
    return (
        cross_top.T,
        sigma_top.T,
        jnp.transpose(cross_kids, (0, 2, 1)),
        jnp.transpose(sigma_kids, (0, 2, 1)),
    )


def solution(mesh):
    fine = Mesh(mesh.devices.reshape(8, 4, 2, 4, 2), ("y", "x", "h", "q", "c"))
    cols = ("x", "h", "q", "c")
    flat = P("y", cols)
    kids = P(None, "y", cols)
    return jax.shard_map(
        per_device,
        mesh=fine,
        in_specs=(flat, flat, flat, P(), kids, kids, P()),
        out_specs=(flat, flat, kids, kids),
        check_vma=False,
    )
```

```python
import jax
import jax.numpy as jnp
from jax import lax
from jax.sharding import Mesh
from jax.sharding import PartitionSpec as P

BLK = 32
LIVE = 16
HIGH = lax.Precision.HIGH
WIN = ("x", "h")
SUB = ("q", "c")


def dot_nt(a, b):
    return lax.dot_general(
        a, b, (((1,), (1,)), ((), ())), precision=HIGH, preferred_element_type=jnp.float32
    )


def pieces(value):
    high = lax.reduce_precision(value, 8, 7)
    rest = value - high
    mid = lax.reduce_precision(rest, 8, 7)
    return [part.astype(jnp.bfloat16) for part in (high, mid, rest - mid)]


def select_exact(value, choice):
    rows = value.shape[0]
    stacked = jnp.concatenate(pieces(value), axis=0)
    picked = lax.dot_general(
        stacked, choice, (((1,), (0,)), ((), ())), preferred_element_type=jnp.float32
    )
    return picked[:rows] + (picked[rows : 2 * rows] + picked[2 * rows :])


def slot_choice(window, block_ids, count):
    order = jnp.arange(window.shape[0])
    rank = jnp.sum(jnp.where(order[None, :] < order[:, None], window[None, :], 0), axis=1)
    slot = jnp.where(window == 1, rank, -1)
    slot_of = jnp.sum(
        jnp.where(block_ids[:, None] == jnp.arange(window.shape[0])[None, :], slot[None, :], 0), axis=1
    )
    slot_of = jnp.broadcast_to(slot_of[:, None], (block_ids.shape[0], BLK)).reshape(-1)
    place = slot_of * BLK + jnp.arange(block_ids.shape[0] * BLK, dtype=jnp.int32) % BLK
    place = jnp.where(slot_of >= 0, place, -1)
    return (place[:, None] == jnp.arange(count, dtype=jnp.int32)[None, :]).astype(jnp.bfloat16)


def swap(value, axis):
    return lax.ppermute(value, axis, [(0, 1), (1, 0)])


def sum_over(parts, axis):
    return jnp.sum(lax.all_to_all(parts, axis, 0, 0, tiled=True), axis=0)


def shift(value, goes, count):
    order = []
    for i in range(count):
        for j in range(count):
            to_y, to_window = goes(i, j)
            order.append((i * count + j, to_y * count + to_window))
    return lax.ppermute(value, ("y",) + WIN, order)


def in_order(parts, first):
    twice = jnp.concatenate([parts, parts], axis=0)
    return lax.dynamic_slice_in_dim(twice, first, parts.shape[0], 0)


def spread(value, axis):
    copies = jnp.broadcast_to(value[None], (lax.axis_size(axis),) + value.shape)
    return lax.all_to_all(copies, axis, 0, 0, tiled=True)


def gather_sub(rows):
    lines = spread(rows, "q")
    both = lax.all_gather(lines, "c", axis=1)
    return both.reshape((-1,) + rows.shape)


def per_device(sigma_anc, panel_top, pivot_top, flags_top, panel_kids, pivot_kids, flags_kids):
    ny, nx, nh = lax.axis_size("y"), lax.axis_size("x"), lax.axis_size("h")
    nq = lax.axis_size("q")
    y_id, q_id, c_id, h_id = (lax.axis_index(a) for a in ("y", "q", "c", "h"))
    win_id = lax.axis_index("x") * nh + h_id
    sub_id = q_id * 2 + c_id
    anc_own, anc_col = sigma_anc.shape
    per_win = anc_own // BLK
    per_col = anc_col // BLK
    live = LIVE * BLK
    top_col = panel_top.shape[1]
    kid_own = panel_kids.shape[1]
    kid_col = panel_kids.shape[2]

    row_window = lax.dynamic_slice_in_dim(flags_top, y_id * per_win, per_win)
    col_window = lax.dynamic_slice_in_dim(flags_top, win_id * per_win, per_win)
    row_choice = slot_choice(row_window, jnp.arange(per_win), live)
    group = jnp.arange(nq * per_col) // per_col
    within = jnp.arange(nq * per_col) % per_col
    near_choice = slot_choice(col_window, (group * 2 + c_id) * per_col + within, live)
    far_choice = slot_choice(col_window, (group * 2 + 1 - c_id) * per_col + within, live)
    own_choice = slot_choice(col_window, sub_id * per_col + jnp.arange(per_col), live)

    packed = select_exact(jnp.concatenate([sigma_anc.T, panel_top.T], axis=0), row_choice)
    field = packed[:anc_col]
    top_rows = packed[anc_col:]
    kid_blocks = kid_own // BLK
    kid_flags = lax.dynamic_slice_in_dim(flags_kids, y_id * kid_blocks, kid_blocks, 1)
    keep_rows = jnp.repeat(kid_flags, BLK, axis=1).astype(jnp.float32)
    kids = jnp.transpose(panel_kids, (0, 2, 1)) * keep_rows[:, None, :]
    panel = jnp.concatenate([top_rows, kids.reshape(2 * kid_col, kid_own)], axis=1)

    kid_rows = lax.all_gather(kids, WIN + SUB, axis=1, tiled=True)
    turned = shift(panel, lambda i, j: ((i + j) % ny, j), ny)
    other = swap(top_rows, "h")
    field, other = lax.optimization_barrier((field, other))
    pair = jnp.stack([jnp.where(h_id == 0, top_rows, other), jnp.where(h_id == 0, other, top_rows)])
    top_wide = spread(pair, "x").reshape(ny * top_col, live)
    turned = shift(turned, lambda i, j: (i, (i - j) % ny), ny)
    near = lax.all_gather(field, "q", axis=0).reshape(nq * anc_col, live)
    near, top_wide, turned = lax.optimization_barrier((near, top_wide, turned))
    far = swap(near, "c")
    copies = jnp.broadcast_to(turned[None], (ny,) + turned.shape)
    zed = jnp.concatenate([dot_nt(top_wide, near), dot_nt(top_wide, far)], axis=1)
    zed = select_exact(zed, jnp.concatenate([near_choice, far_choice], axis=0))
    zed = sum_over(zed.reshape(ny, top_col, live), "y")
    zed, copies = lax.optimization_barrier((zed, copies))
    turned = lax.all_to_all(copies, "y", 0, 0, tiled=True).reshape(ny * top_col, live + kid_own)
    zed = lax.all_gather(lax.all_gather(zed, "q", axis=0), "c", axis=1).reshape(-1, live)
    cross_top = -lax.dot_general(
        own_choice, jnp.concatenate(pieces(zed), axis=0), (((1,), (1,)), ((), ())),
        preferred_element_type=jnp.float32,
    ).reshape(anc_col, 3, -1).sum(axis=1)

    part = dot_nt(turned[:, :live], zed)
    part, kid_rows = lax.optimization_barrier((part, kid_rows))
    kid_high, kid_low, _ = pieces(kid_rows.reshape(-1, kid_own))
    kid_terms = jnp.concatenate([kid_high, kid_low, kid_high], axis=1)
    sigma_top = pivot_top.T + sum_over(
        in_order(part.reshape(nx * nh, top_col, -1), win_id), WIN
    )

    top_high, top_low, _ = pieces(sigma_top)
    part = lax.dot_general(
        jnp.concatenate([top_high, top_high, top_low], axis=1),
        kid_terms,
        (((1,), (1,)), ((), ())),
        preferred_element_type=jnp.float32,
    ).reshape(top_col, 2, ny, -1)
    zed = sum_over(jnp.transpose(part, (2, 1, 0, 3)), "y")
    col_flags = lax.dynamic_slice_in_dim(flags_kids, win_id * kid_blocks + sub_id, 1, 1)
    cross_kids = -(zed * col_flags.astype(jnp.float32)[:, :, None])

    zed = gather_sub(zed)
    turned_kids = turned[:, live:].reshape(nx * nh, 2, kid_col, kid_own)
    part = jnp.stack(
        [
            lax.dot(
                turned_kids[:, k].reshape(-1, kid_own),
                zed[:, k].reshape(kid_own, -1),
                precision=HIGH,
                preferred_element_type=jnp.float32,
            )
            for k in range(2)
        ]
    )
    part = jnp.transpose(part.reshape(2, nx * nh, kid_col, -1), (1, 0, 2, 3))
    sigma_kids = jnp.transpose(pivot_kids, (0, 2, 1)) + sum_over(in_order(part, win_id), WIN)
    return (
        cross_top.T,
        sigma_top.T,
        jnp.transpose(cross_kids, (0, 2, 1)),
        jnp.transpose(sigma_kids, (0, 2, 1)),
    )


def solution(mesh):
    fine = Mesh(mesh.devices.reshape(8, 4, 2, 4, 2), ("y", "x", "h", "q", "c"))
    cols = ("x", "h", "q", "c")
    flat = P("y", cols)
    kids = P(None, "y", cols)
    return jax.shard_map(
        per_device,
        mesh=fine,
        in_specs=(flat, flat, flat, P(), kids, kids, P()),
        out_specs=(flat, flat, kids, kids),
        check_vma=False,
    )
```
